32 devices in a mesh: seq: 4 (over z), col: 4 (over x, core), batch: 2 (over y).
Axes of the slice: x: 2, y: 2, z: 4, core: 2. Of those that a mesh axis runs over, the one named last changes fastest.
Arguments:
- tokens: int32 [2, 262144], P('batch', ('seq', 'col')), may hold values from 0 to 3
- stem_weight: bfloat16 [64, 768], replicated, may hold values from -1.5 to 1.5
- conv_weight: bfloat16 [3840, 768], replicated, may hold values from -0.09375 to 0.09375
- conv_bias: float32 [768], replicated, may hold values from -1 to 1
- up_weight: bfloat16 [768, 1536], replicated, may hold values from -0.21875 to 0.21875
- norm_gain: float32 [1536], replicated, may hold values from 0.1 to 1.9
- pair_weight: bfloat16 [1536, 64], replicated, may hold values from -0.15625 to 0.15625
- out_weight: bfloat16 [1024, 128], replicated, may hold values from -0.1875 to 0.1875
- cotangent: bfloat16 [2, 128, 128, 128], P('batch', 'seq', 'col'), may hold values from -24 to 24
- projection: float32 [768, 128], replicated, may hold values from -0.21875 to 0.21875
- buckets: int32 [3840], replicated, may hold values from 0 to 31
Outputs:
- input_grad: bfloat16 [2, 16384, 768], P('batch', ('seq', 'col'))
- embedding: float32 [2, 32, 128], P('batch')
The draws below stay inside these ranges and needn't reach their ends.
All inputs are finite; a program needn't handle non-finite values.
Results may differ from the reference program's by a relative error of at most 0.012.
Values may be sent and summed in bfloat16 or wider, within the bound.
A program may use at most 128 MiB of HBM per device.

```python
import jax
import jax.numpy as jnp
from jax import lax

C = 768
CB = 1536
PC = 128
OP = 32
KERNEL = 5
PATCH = 16
POOL = 128
BUCKETS = 32
PROJ = 128
B = 2
BINS = 128
FINE = 16384
BP = 262144
ROWB = 32


def with_ends(result, own_key, smallest, high):
    longest = result.shape.index(max(result.shape))
    spots = []
    for shift in (0, 1):
        where = [jax.random.randint(jax.random.fold_in(own_key, axis), (), 0, length) for axis, length in enumerate(result.shape)]
        where[longest] = (where[longest] + shift) % result.shape[longest]
        spots.append(tuple(where))
    return result.at[spots[0]].set(smallest).at[spots[1]].set(high)


def block_levels(rng, extent, shards, least, largest):
    factor_of, own = 1.0, jax.random.fold_in(rng, 6)
    for axis_at, blocks in shards:
        heights = jnp.exp(jax.random.uniform(jax.random.fold_in(own, axis_at), (blocks,), jnp.float32, least / len(shards), largest / len(shards)))
        factor_of = factor_of * jnp.repeat(heights, extent[axis_at] // blocks).reshape([-1 if axis == axis_at else 1 for axis in range(len(extent))])
    return factor_of


def bell_draw(rng, dims, scale, most, cuts=(), kind=jnp.bfloat16):
    drawn = jax.random.normal(rng, dims, jnp.float32) * scale
    if len(cuts) > 0:
        drawn = block_levels(rng, dims, cuts, -0.22, 0.18) * drawn
    return jnp.clip(drawn, min=-most, max=most).astype(kind)


def setup_inputs(seed: int = 0) -> dict:
    splits = jax.random.split(jax.random.key(seed), 12)
    return {
        "tokens": with_ends(jax.random.randint(splits[0], (B, BP), 0, 4), jax.random.fold_in(splits[0], 1), 0, 3).astype(jnp.int32),
        "stem_weight": bell_draw(splits[1], (PATCH * 4, C), PATCH ** -0.5, 1.5),
        "conv_weight": bell_draw(splits[2], (KERNEL * C, C), (KERNEL * C) ** -0.5, 0.09375),
        "conv_bias": jnp.clip(jax.random.uniform(splits[3], (C,), jnp.float32, -1.0, 1.0), -1.0, 1.0),
        "up_weight": bell_draw(splits[4], (C, CB), C ** -0.5, 0.21875),
        "norm_gain": jnp.clip(1.0 + 0.18 * jax.random.normal(splits[5], (CB,), jnp.float32), 0.1, 1.9),
        "pair_weight": bell_draw(splits[6], (CB, 2 * OP), CB ** -0.5, 0.15625),
        "out_weight": bell_draw(splits[7], (OP * OP, PC), (OP * OP) ** -0.5, 0.1875),
        "cotangent": bell_draw(splits[8], (B, BINS, BINS, PC), 4.0, 24.0, ((0, 2), (1, 4), (2, 4))),
        "projection": bell_draw(splits[9], (C, PROJ), C ** -0.5, 0.21875, (), jnp.float32),
        "buckets": with_ends(jax.random.randint(splits[10], (KERNEL * C,), 0, BUCKETS), jax.random.fold_in(splits[10], 1), 0, BUCKETS - 1).astype(jnp.int32),
    }


highest = lax.Precision.HIGHEST

def one_interval(bases, stem_weight, conv_weight, conv_bias, up_weight, norm_gain, pair_weight, out_weight, grid, projection, buckets):
    reach = (KERNEL - 1) // 2
    onehot = (bases.reshape(FINE, PATCH)[:, :, None] == jnp.arange(4, dtype=jnp.int32)).astype(jnp.bfloat16).reshape(FINE, PATCH * 4)
    embedded = jnp.dot(onehot, stem_weight, preferred_element_type=jnp.float32).astype(jnp.bfloat16)
    padded = jnp.pad(embedded, ((reach, reach), (0, 0)))
    taps = conv_weight.reshape(KERNEL, C, C)
    before = jnp.zeros((FINE, C), jnp.float32) + conv_bias
    for offset in range(KERNEL):
        before = before + jnp.dot(padded[offset:offset + FINE], taps[offset], preferred_element_type=jnp.float32)
    after, gelu_back = jax.vjp(jax.nn.gelu, before)
    pooled = lax.optimization_barrier(jnp.mean(after.reshape(BINS, POOL, C), axis=1)).astype(jnp.bfloat16)
    hidden = jnp.dot(pooled, up_weight, preferred_element_type=jnp.float32)
    inverse = lax.rsqrt(lax.optimization_barrier(jnp.mean(hidden * hidden, axis=1, keepdims=True)) + 1e-06)
    normed = (hidden * inverse * norm_gain).astype(jnp.bfloat16)
    left = jnp.dot(normed, pair_weight[:, :OP], preferred_element_type=jnp.float32).astype(jnp.bfloat16)
    right = jnp.dot(normed, pair_weight[:, OP:], preferred_element_type=jnp.float32).astype(jnp.bfloat16)
    groups = BINS // ROWB
    blocks = grid.reshape(groups, ROWB, BINS, PC)
    left_groups = left.astype(jnp.float32).reshape(groups, ROWB, OP)
    right_wide = right.astype(jnp.float32)

    def pair_step(carry, inputs):
        block, rows_left = inputs
        outer_grad = lax.dot_general(block.reshape(ROWB * BINS, PC), out_weight, (((1,), (1,)), ((), ())), preferred_element_type=jnp.float32).reshape(ROWB, BINS, OP, OP)
        grad_left = jnp.einsum('ijkl,jl->ik', outer_grad, right_wide, precision=highest)
        carry = carry + jnp.einsum('ijkl,ik->jl', outer_grad, rows_left, precision=highest)
        return (carry, grad_left)
    grad_right, grad_left = lax.scan(pair_step, jnp.zeros((BINS, OP), jnp.float32), (blocks, left_groups))
    grad_left = grad_left.reshape(BINS, OP)
    both_grads = jnp.concatenate([grad_left, grad_right], axis=1)
    d_normed = lax.dot_general(both_grads, pair_weight.astype(jnp.float32), (((1,), (1,)), ((), ())), precision=highest)
    scaled = d_normed * norm_gain
    inner = lax.optimization_barrier(jnp.mean(scaled * hidden, axis=1, keepdims=True))
    d_hidden = inverse * scaled - hidden * inverse ** 3 * inner
    d_pooled = lax.dot_general(d_hidden, up_weight.astype(jnp.float32), (((1,), (1,)), ((), ())), precision=highest)
    spread = jnp.broadcast_to(d_pooled[:, None, :] / POOL, (BINS, POOL, C)).reshape(FINE, C)
    d_before = gelu_back(spread)[0].astype(jnp.bfloat16)
    grads_padded = jnp.pad(d_before, ((reach, reach), (0, 0)))
    input_grad = jnp.zeros((FINE, C), jnp.float32)
    for offset in range(KERNEL):
        first = 2 * reach - offset
        input_grad = input_grad + lax.dot_general(grads_padded[first:first + FINE], taps[offset], (((1,), (1,)), ((), ())), preferred_element_type=jnp.float32)
    weight_grad = jnp.concatenate([lax.dot_general(padded[offset:offset + FINE], d_before, (((0,), (0,)), ((), ())), preferred_element_type=jnp.float32) for offset in range(KERNEL)], axis=0)
    member = (buckets[None, :] == jnp.arange(BUCKETS, dtype=jnp.int32)[:, None]).astype(jnp.float32)
    sketch = jnp.dot(member, jnp.dot(weight_grad, projection, precision=highest), precision=highest)
    unit = sketch * lax.rsqrt(jnp.mean(sketch * sketch) + 1e-06)
    return (input_grad.astype(jnp.bfloat16), unit)

def reference(tokens, stem_weight, conv_weight, conv_bias, up_weight, norm_gain, pair_weight, out_weight, cotangent, projection, buckets):
    grads_list = []
    units_list = []
    for interval in range(B):
        grads_one, unit_one = one_interval(tokens[interval], stem_weight, conv_weight, conv_bias, up_weight, norm_gain, pair_weight, out_weight, cotangent[interval], projection, buckets)
        grads_list.append(grads_one)
        units_list.append(unit_one)
    units = jnp.stack(units_list, axis=0)
    center = lax.optimization_barrier(jnp.sum(units, axis=0)) / B
    return (jnp.stack(grads_list, axis=0), units - center[None])
```

```python
import functools

import jax
import jax.numpy as jnp
from jax import lax
from jax.experimental import pallas as pl
from jax.experimental.pallas import tpu as pltpu
from jax.sharding import PartitionSpec as P

OP = 32
PATCH = 16
POOL = 128
BUCKETS = 32
BASES = 4
LANES = 128
PAD = 8

MESH = pl.DeviceIdType.MESH
F32 = jnp.float32
BF16 = jnp.bfloat16


def nn(a, b):
    return lax.dot_general(a, b, (((1,), (0,)), ((), ())), preferred_element_type=F32)


def nt(a, b):
    return lax.dot_general(a, b, (((1,), (1,)), ((), ())), preferred_element_type=F32)


def halves(values):
    upper = values.astype(BF16)
    lower = (values - upper.astype(F32)).astype(BF16)
    return jnp.concatenate([upper, lower], axis=0)


def joined(values):
    rows = values.shape[0] // 2
    return values[:rows] + values[rows:]


def iota(shape, dim):
    return lax.broadcasted_iota(jnp.int32, shape, dim)


def body(
    counts,
    tok,
    stem,
    bias,
    gain,
    pair,
    proj,
    buck,
    conv_h,
    up_h,
    outw_h,
    cot_h,
    out_h,
    emb,
    conv,
    up,
    outw,
    cot,
    grid,
    seen,
    hot,
    mixed,
    slope,
    pool,
    dpad,
    outv,
    halo_tok,
    lr,
    got_left,
    got_right,
    part_left,
    part_right,
    sum_left,
    sum_right,
    marks,
    sk,
    sk_a,
    sk_b,
    sk_bsrc,
    sk_c,
    sk_csrc,
    load_sem,
    store_sem,
    tok_send,
    tok_recv,
    left_send,
    left_recv,
    right_send,
    right_recv,
    gl_send,
    gl_recv,
    gr_send,
    gr_recv,
    edge_send,
    edge_recv,
    a_send,
    a_recv,
    b_send,
    b_recv,
    c_send,
    c_recv,
):
    seq_n, col_n, batch_n = counts
    seq, col, bat = lax.axis_index("seq"), lax.axis_index("col"), lax.axis_index("batch")
    me = seq * col_n + col
    last = seq_n * col_n - 1
    channels = conv.shape[1]
    kernel = conv.shape[0] // channels
    reach = (kernel - 1) // 2
    patches = slope.shape[0]
    bins = patches // POOL
    width = stem.shape[0]
    rows_n, cols_n = bins * col_n, bins * seq_n

    loads = [
        pltpu.make_async_copy(src, dst, load_sem.at[at])
        for at, (src, dst) in enumerate(((conv_h, conv), (up_h, up), (outw_h, outw), (cot_h, cot)))
    ]
    for load in loads:
        load.start()

    def place(linear):
        return {"seq": lax.div(linear, col_n), "col": lax.rem(linear, col_n), "batch": bat}

    def at(s, c, b):
        return {"seq": s, "col": c, "batch": b}

    def remote(src, dst, send, recv, device):
        return pltpu.make_async_remote_copy(
            src_ref=src,
            dst_ref=dst,
            send_sem=send,
            recv_sem=recv,
            device_id=device,
            device_id_type=MESH,
        )

    barrier = pltpu.get_barrier_semaphore()
    for step in range(1, seq_n * col_n):
        pl.semaphore_signal(
            barrier,
            inc=1,
            device_id=place(lax.rem(me + step, seq_n * col_n)),
            device_id_type=MESH,
        )
    for b_step in range(1, batch_n):
        for c_step in range(col_n):
            pl.semaphore_signal(
                barrier,
                inc=1,
                device_id=at(seq, lax.rem(col + c_step, col_n), lax.rem(bat + b_step, batch_n)),
                device_id_type=MESH,
            )

    spread = (lax.rem(iota((LANES, LANES), 0), PATCH) == lax.div(lax.rem(iota((LANES, LANES), 1), width), BASES)).astype(BF16)

    def expand(lines):
        count = lines.shape[0]
        wide = jnp.broadcast_to(lines.astype(F32)[:, None, :], (count, PAD, LANES)).reshape(count * PAD, LANES)
        own = lax.div(iota(wide.shape, 1), PATCH) == lax.rem(iota(wide.shape, 0), PAD)
        return nn(jnp.where(own, wide, 0.0).astype(BF16), spread)

    seen[pl.ds(PAD, patches), :] = expand(tok[...])
    mixed[pl.ds(kernel * width, width), :] = jnp.zeros((width, channels), BF16)

    pl.semaphore_wait(barrier, seq_n * col_n - 1 + (batch_n - 1) * col_n)

    lines_n = tok.shape[0]
    to_left = remote(tok.at[pl.ds(0, PAD)], halo_tok.at[1], tok_send.at[0], tok_recv.at[1], place(jnp.maximum(me - 1, 0)))
    to_right = remote(tok.at[pl.ds(lines_n - PAD, PAD)], halo_tok.at[0], tok_send.at[1], tok_recv.at[0], place(jnp.minimum(me + 1, last)))

    @pl.when(me > 0)
    def _():
        to_left.start()

    @pl.when(me < last)
    def _():
        to_right.start()

    loads[0].wait()
    for k in range(kernel):
        mixed[pl.ds(k * width, width), :] = nn(stem[...], conv[pl.ds(k * channels, channels), :]).astype(BF16)

    @pl.when(me > 0)
    def _():
        to_left.wait_send()
        to_right.wait_recv()
        seen[pl.ds(0, PAD), :] = expand(halo_tok[0, PAD - 1 : PAD, :])

    @pl.when(me == 0)
    def _():
        seen[pl.ds(0, PAD), :] = jnp.full((PAD, LANES), -1.0, F32)

    @pl.when(me < last)
    def _():
        to_right.wait_send()
        to_left.wait_recv()
        seen[pl.ds(PAD + patches, PAD), :] = expand(halo_tok[1, 0:1, :])

    @pl.when(me == last)
    def _():
        seen[pl.ds(PAD + patches, PAD), :] = jnp.full((PAD, LANES), -1.0, F32)

    lane = iota((patches, LANES), 1)
    base = lax.rem(lane, BASES).astype(F32)
    for group in range((kernel + 1) // 2):
        first = PAD - reach + 2 * group
        low = seen[pl.ds(first, patches), :]
        if 2 * group + 1 < kernel:
            high = seen[pl.ds(first + 1, patches), :]
        else:
            high = -1.0
        hot[:, group * LANES : (group + 1) * LANES] = jnp.where(jnp.where(lane < width, low, high) == base, 1.0, 0.0).astype(BF16)

    root = 0.7978845608028654
    cube = root * 0.044715

    @pl.loop(0, bins)
    def _(b):
        rows = pl.ds(pl.multiple_of(b * POOL, POOL), POOL)
        v = nn(hot[rows, :], mixed[...]) + bias[...]
        square = v * v
        t = jnp.tanh(v * (root + cube * square))
        half = 0.5 + 0.5 * t
        pool[pl.ds(b, 1), :] = jnp.sum(v * half, axis=0, keepdims=True) * (1.0 / POOL)
        slope[rows, :] = (half + 0.5 * v * (1.0 - t * t) * (root + 3.0 * cube * square)) * (1.0 / POOL)

    loads[1].wait()
    hidden = nn(pool[...].astype(BF16), up[...])
    inverse = lax.rsqrt(jnp.mean(hidden * hidden, axis=1, keepdims=True) + 1e-06)
    normed = (hidden * inverse * gain[...]).astype(BF16)
    lr[...] = jnp.zeros(lr.shape, F32)
    lr[:, : 2 * OP] = nn(normed, pair[...]).astype(BF16).astype(F32)

    user = lax.div(me, seq_n)
    slot = lax.rem(me, seq_n)
    lefts, rights = [], []
    for step in range(1, col_n):
        peer = lax.rem(col + step, col_n)
        lefts.append(remote(lr, got_left.at[col], left_send.at[step], left_recv.at[col], at(seq, peer, bat)))
        lefts[-1].start()
    for s in range(seq_n):
        copy = remote(lr, got_right.at[slot], right_send.at[s], right_recv.at[slot], at(s, user, bat))
        rights.append((copy, (seq != s) | (col != user)))

        @pl.when(rights[-1][1])
        def _():
            copy.start()

    got_left[col] = lr[...]

    @pl.when(col == user)
    def _():
        got_right[slot] = lr[...]

    loads[2].wait()
    loads[3].wait()
    step_rows = 2 * LANES

    @pl.loop(0, rows_n * cols_n // step_rows)
    def _(i):
        rows = pl.ds(pl.multiple_of(i * step_rows, step_rows), step_rows)
        grid[rows, :] = nt(cot[rows, :], outw[...])

    for step in range(1, col_n):
        peer = lax.rem(col + step, col_n)
        remote(lr, got_left.at[peer], left_send.at[step], left_recv.at[peer], at(seq, peer, bat)).wait_recv()
    for s in range(seq_n):
        owner = col * seq_n + s

        @pl.when(owner != me)
        def _():
            remote(lr, got_right.at[s], right_send.at[s], right_recv.at[s], place(owner)).wait_recv()

    for copy in lefts:
        copy.wait_send()
    for copy, other in rights:

        @pl.when(other)
        def _():
            copy.wait_send()

    outer = OP * OP
    pick_left = (iota((LANES, outer), 0) == lax.div(iota((LANES, outer), 1), OP)).astype(BF16)
    pick_right = (iota((LANES, outer), 0) == OP + lax.rem(iota((LANES, outer), 1), OP)).astype(BF16)
    wide_left = nn(got_left[...].reshape(rows_n, LANES).astype(BF16), pick_left)
    wide_right = nn(got_right[...].reshape(cols_n, LANES).astype(BF16), pick_right)
    over_cols, over_rows = [], []
    for tile in range(outer // LANES):
        lanes = slice(tile * LANES, (tile + 1) * LANES)
        cells = grid[:, lanes].reshape(rows_n, cols_n, LANES)
        over_cols.append(jnp.sum(cells * wide_right[None, :, lanes], axis=1))
        over_rows.append(jnp.sum(cells * wide_left[:, None, lanes], axis=0))
    part_left[...] = joined(nt(halves(jnp.concatenate(over_cols, axis=1)), pick_left))
    part_right[...] = joined(nt(halves(jnp.concatenate(over_rows, axis=1)), pick_right))

    lefts, rights = [], []
    for step in range(1, col_n):
        peer = lax.rem(col + step, col_n)
        piece = part_left.at[pl.ds(pl.multiple_of(peer * bins, bins), bins)]
        lefts.append(remote(piece, sum_left.at[col], gl_send.at[step], gl_recv.at[col], at(seq, peer, bat)))
        lefts[-1].start()
    for s in range(seq_n):
        owner = col * seq_n + s
        copy = remote(part_right.at[pl.ds(s * bins, bins)], sum_right.at[seq], gr_send.at[s], gr_recv.at[seq], place(owner))
        rights.append((copy, owner != me))

        @pl.when(owner != me)
        def _():
            copy.start()

        @pl.when(owner == me)
        def _():
            sum_right[seq] = part_right[s * bins : (s + 1) * bins, :]

    sum_left[col] = part_left[pl.ds(pl.multiple_of(col * bins, bins), bins), :]

    member = (buck[...] == iota((BUCKETS, kernel * channels), 0)).astype(BF16)
    stems = [nt(member[:, k * channels : (k + 1) * channels], stem[...]) for k in range(kernel)]
    stems.append(jnp.zeros((BUCKETS, width), F32))
    marks[...] = halves(joined(nt(halves(jnp.concatenate(stems, axis=1)), hot[...])))

    for step in range(1, col_n):
        peer = lax.rem(col + step, col_n)
        remote(lr, sum_left.at[peer], gl_send.at[step], gl_recv.at[peer], at(seq, peer, bat)).wait_recv()
    for s in range(seq_n):

        @pl.when((seq != s) | (col != user))
        def _():
            remote(lr, sum_right.at[s], gr_send.at[s], gr_recv.at[s], at(s, user, bat)).wait_recv()

    both = jnp.sum(sum_left[...], axis=0) + jnp.sum(sum_right[...], axis=0)
    d_normed = joined(nt(halves(both[:, : 2 * OP]), pair[...]))
    scaled = d_normed * gain[...]
    inner = jnp.mean(scaled * hidden, axis=1, keepdims=True)
    d_hidden = inverse * scaled - hidden * (inverse * inverse * inverse) * inner
    pool[...] = joined(nt(halves(d_hidden), up[...]))

    dpad[pl.ds(PAD, PAD), :] = slope[:PAD, :] * pool[0:1, :]
    dpad[pl.ds(patches, PAD), :] = slope[patches - PAD :, :] * pool[bins - 1 : bins, :]
    edge_left = remote(dpad.at[pl.ds(PAD, PAD)], dpad.at[pl.ds(PAD + patches, PAD)], edge_send.at[0], edge_recv.at[1], place(jnp.maximum(me - 1, 0)))
    edge_right = remote(dpad.at[pl.ds(patches, PAD)], dpad.at[pl.ds(0, PAD)], edge_send.at[1], edge_recv.at[0], place(jnp.minimum(me + 1, last)))

    @pl.when(me > 0)
    def _():
        edge_left.start()

    @pl.when(me < last)
    def _():
        edge_right.start()

    @pl.when(me == 0)
    def _():
        dpad[pl.ds(0, PAD), :] = jnp.zeros((PAD, channels), F32)

    @pl.when(me == last)
    def _():
        dpad[pl.ds(PAD + patches, PAD), :] = jnp.zeros((PAD, channels), F32)

    for copy in lefts:
        copy.wait_send()
    for copy, other in rights:

        @pl.when(other)
        def _():
            copy.wait_send()

    total = jnp.zeros((2 * BUCKETS, channels), F32)
    for b in range(bins):
        first = b * POOL
        cells = slope[first : first + POOL, :] * pool[b : b + 1, :]
        low = PAD if b == 0 else 0
        high = POOL - PAD if b == bins - 1 else POOL
        dpad[pl.ds(PAD + first + low, high - low), :] = cells[low:high]
        total = total + nn(marks[:, first : first + POOL], cells.astype(BF16))
    sk[...] = lax.dot_general(
        joined(total), proj[...], (((1,), (0,)), ((), ())), precision=lax.Precision.HIGHEST, preferred_element_type=F32
    )
    share = BUCKETS // col_n

    sends_a = []
    for step in range(1, col_n):
        peer = lax.rem(col + step, col_n)
        piece = sk.at[pl.ds(pl.multiple_of(peer * share, share), share)]
        sends_a.append(remote(piece, sk_a.at[col], a_send.at[step], a_recv.at[col], at(seq, peer, bat)))
        sends_a[-1].start()
    sk_a[col] = sk[pl.ds(pl.multiple_of(col * share, share), share), :]
    sends_b = [
        remote(sk_bsrc, sk_b.at[seq], b_send.at[step], b_recv.at[seq], at(lax.rem(seq + step, seq_n), col, bat))
        for step in range(1, seq_n)
    ]
    pairs = [(b, c) for b in range(batch_n) for c in range(col_n) if b + c > 0]
    sends_c = [
        remote(
            sk_csrc,
            sk_c.at[bat, col],
            c_send.at[b, c],
            c_recv.at[bat, col],
            at(seq, lax.rem(col + c, col_n), lax.rem(bat + b, batch_n)),
        )
        for b, c in pairs
    ]

    chunk = 2 * LANES
    chunks = patches // chunk

    @pl.loop(0, chunks)
    def _(i):
        @pl.when(i == 1)
        def _():
            for step in range(1, col_n):
                peer = lax.rem(col + step, col_n)
                remote(sk_bsrc, sk_a.at[peer], a_send.at[step], a_recv.at[peer], at(seq, peer, bat)).wait_recv()
            sk_bsrc[...] = jnp.sum(sk_a[...], axis=0)
            sk_b[seq] = jnp.sum(sk_a[...], axis=0)
            for copy in sends_b:
                copy.start()

        @pl.when(i == 2)
        def _():
            for step in range(1, seq_n):
                peer = lax.rem(seq + step, seq_n)
                remote(sk_bsrc, sk_b.at[peer], b_send.at[step], b_recv.at[peer], at(peer, col, bat)).wait_recv()
            sk_csrc[...] = jnp.sum(sk_b[...], axis=0)
            sk_c[bat, col] = jnp.sum(sk_b[...], axis=0)
            for copy in sends_c:
                copy.start()

            @pl.when(me > 0)
            def _():
                edge_left.wait_send()
                edge_right.wait_recv()

            @pl.when(me < last)
            def _():
                edge_right.wait_send()
                edge_left.wait_recv()

        spot = lax.rem(i + 1, chunks)
        begin = pl.multiple_of(spot * chunk, chunk)
        wide = dpad[pl.ds(begin, chunk + 2 * PAD), :]
        acc = jnp.zeros((chunk, channels), F32)
        for k in range(kernel):
            shift = PAD + reach - k
            acc = acc + nt(wide[shift : shift + chunk].astype(BF16), conv[pl.ds(k * channels, channels), :])
        outv[pl.ds(begin, chunk), :] = acc.astype(BF16)
        pltpu.make_async_copy(outv.at[pl.ds(begin, chunk)], out_h.at[pl.ds(begin, chunk)], store_sem.at[spot]).start()

    for b, c in pairs:
        other_b, other_c = lax.rem(bat + b, batch_n), lax.rem(col + c, col_n)
        remote(sk_csrc, sk_c.at[other_b, other_c], c_send.at[b, c], c_recv.at[other_b, other_c], at(seq, other_c, other_b)).wait_recv()

    def unit(values):
        values = values.reshape(BUCKETS, values.shape[-1])
        return values * lax.rsqrt(jnp.mean(values * values) + 1e-06)

    center = unit(sk_c[0])
    for b in range(1, batch_n):
        center = center + unit(sk_c[b])
    emb[...] = unit(sk_c[bat]) - center * (1.0 / batch_n)
    for copy in sends_a + sends_b + sends_c:
        copy.wait_send()
    for i in range(chunks):
        rows = pl.ds(i * chunk, chunk)
        pltpu.make_async_copy(outv.at[rows], out_h.at[rows], store_sem.at[i]).wait()


def shards(
    tokens,
    stem_weight,
    conv_weight,
    conv_bias,
    up_weight,
    norm_gain,
    pair_weight,
    out_weight,
    cotangent,
    projection,
    buckets,
):
    seq_n, col_n, batch_n = (lax.axis_size(axis) for axis in ("seq", "col", "batch"))
    channels = conv_weight.shape[1]
    kernel = conv_weight.shape[0] // channels
    patches = tokens.shape[1] // PATCH
    bins = patches // POOL
    rows_n, cols_n = bins * col_n, bins * seq_n
    proj_n = projection.shape[1]
    share = BUCKETS // col_n
    hot_n = (kernel + 1) // 2 * LANES
    vmem = pl.BlockSpec(memory_space=pltpu.VMEM)
    hbm = pl.BlockSpec(memory_space=pl.ANY)
    dma = pltpu.SemaphoreType.DMA
    cot = cotangent.reshape(rows_n * cols_n, cotangent.shape[3])
    scratch = [
        pltpu.VMEM(conv_weight.shape, BF16),
        pltpu.VMEM(up_weight.shape, BF16),
        pltpu.VMEM(out_weight.shape, BF16),
        pltpu.VMEM(cot.shape, BF16),
        pltpu.VMEM((rows_n * cols_n, OP * OP), F32),
        pltpu.VMEM((patches + 2 * PAD, LANES), F32),
        pltpu.VMEM((patches, hot_n), BF16),
        pltpu.VMEM((hot_n, channels), BF16),
        pltpu.VMEM((patches, channels), F32),
        pltpu.VMEM((bins, channels), F32),
        pltpu.VMEM((patches + 2 * PAD, channels), F32),
        pltpu.VMEM((patches, channels), BF16),
        pltpu.VMEM((2, PAD, LANES), jnp.int32),
        pltpu.VMEM((bins, LANES), F32),
        pltpu.VMEM((col_n, bins, LANES), F32),
        pltpu.VMEM((seq_n, bins, LANES), F32),
        pltpu.VMEM((rows_n, LANES), F32),
        pltpu.VMEM((cols_n, LANES), F32),
        pltpu.VMEM((col_n, bins, LANES), F32),
        pltpu.VMEM((seq_n, bins, LANES), F32),
        pltpu.VMEM((2 * BUCKETS, patches), BF16),
        pltpu.VMEM((BUCKETS, proj_n), F32),
        pltpu.VMEM((col_n, share, proj_n), F32),
        pltpu.VMEM((seq_n, share, proj_n), F32),
        pltpu.VMEM((share, proj_n), F32),
        pltpu.VMEM((batch_n, col_n, share, proj_n), F32),
        pltpu.VMEM((share, proj_n), F32),
        dma((4,)),
        dma((patches // (2 * LANES),)),
        dma((2,)),
        dma((2,)),
        dma((col_n,)),
        dma((col_n,)),
        dma((seq_n,)),
        dma((seq_n,)),
        dma((col_n,)),
        dma((col_n,)),
        dma((seq_n,)),
        dma((seq_n,)),
        dma((2,)),
        dma((2,)),
        dma((col_n,)),
        dma((col_n,)),
        dma((seq_n,)),
        dma((seq_n,)),
        dma((batch_n, col_n)),
        dma((batch_n, col_n)),
    ]
    input_grad, embedding = pl.pallas_call(
        functools.partial(body, (seq_n, col_n, batch_n)),
        out_shape=(
            jax.ShapeDtypeStruct((patches, channels), BF16),
            jax.ShapeDtypeStruct((BUCKETS, proj_n), F32),
        ),
        in_specs=[vmem] * 7 + [hbm] * 4,
        out_specs=(hbm, vmem),
        scratch_shapes=scratch,
        compiler_params=pltpu.CompilerParams(
            collective_id=0, has_side_effects=True, vmem_limit_bytes=56 * 2**20
        ),
    )(
        tokens.reshape(patches * PATCH // LANES, LANES),
        stem_weight,
        conv_bias.reshape(1, channels),
        norm_gain.reshape(1, -1),
        pair_weight,
        projection,
        buckets.reshape(1, -1),
        conv_weight,
        up_weight,
        out_weight,
        cot,
    )
    return (input_grad[None], embedding[None])


def solution(mesh):
    in_specs = (
        P("batch", ("seq", "col")),
        P(),
        P(),
        P(),
        P(),
        P(),
        P(),
        P(),
        P("batch", "seq", "col", None),
        P(),
        P(),
    )
    out_specs = (P("batch", ("seq", "col"), None), P("batch", None, None))
    return jax.shard_map(shards, mesh=mesh, in_specs=in_specs, out_specs=out_specs, check_vma=False)
```

```python
import functools

import jax
import jax.numpy as jnp
from jax import lax
from jax.experimental import pallas as pl
from jax.experimental.pallas import tpu as pltpu
from jax.sharding import PartitionSpec as P

OP = 32
PATCH = 16
POOL = 128
BUCKETS = 32
BASES = 4
LANES = 128
PAD = 8

MESH = pl.DeviceIdType.MESH
F32 = jnp.float32
BF16 = jnp.bfloat16


def nn(a, b):
    return lax.dot_general(a, b, (((1,), (0,)), ((), ())), preferred_element_type=F32)


def nt(a, b):
    return lax.dot_general(a, b, (((1,), (1,)), ((), ())), preferred_element_type=F32)


def halves(values):
    upper = values.astype(BF16)
    lower = (values - upper.astype(F32)).astype(BF16)
    return jnp.concatenate([upper, lower], axis=0)


def joined(values):
    rows = values.shape[0] // 2
    return values[:rows] + values[rows:]


def iota(shape, dim):
    return lax.broadcasted_iota(jnp.int32, shape, dim)


def body(
    counts,
    tok_h,
    stem_h,
    bias_h,
    gain_h,
    pair_h,
    proj_h,
    buck_h,
    conv_h,
    up_h,
    outw_h,
    cot_h,
    out_h,
    emb,
    tok,
    stem,
    bias,
    gain,
    pair,
    proj,
    buck,
    conv,
    up,
    outw,
    cot,
    grid,
    seen,
    hot,
    mixed,
    slope,
    pool,
    dpad,
    outv,
    halo_tok,
    lr,
    got_left,
    got_right,
    part_left,
    part_right,
    sum_left,
    sum_right,
    marks,
    sk,
    sk_a,
    sk_b,
    sk_bsrc,
    sk_c,
    sk_csrc,
    load_sem,
    store_sem,
    tok_send,
    tok_recv,
    left_send,
    left_recv,
    right_send,
    right_recv,
    gl_send,
    gl_recv,
    gr_send,
    gr_recv,
    edge_send,
    edge_recv,
    a_send,
    a_recv,
    b_send,
    b_recv,
    c_send,
    c_recv,
):
    seq_n, col_n, batch_n = counts
    seq, col, bat = lax.axis_index("seq"), lax.axis_index("col"), lax.axis_index("batch")
    me = seq * col_n + col
    last = seq_n * col_n - 1
    channels = conv.shape[1]
    kernel = conv.shape[0] // channels
    reach = (kernel - 1) // 2
    patches = slope.shape[0]
    bins = patches // POOL
    width = stem.shape[0]
    rows_n, cols_n = bins * col_n, bins * seq_n

    taps = [pl.ds(k * channels, channels) for k in range(kernel)]
    moves = [(tok_h, tok), (stem_h, stem)]
    moves += [(conv_h.at[tap], conv.at[tap]) for tap in taps]
    moves += [(bias_h, bias), (up_h, up), (gain_h, gain), (pair_h, pair)]
    moves += [(outw_h, outw), (cot_h, cot), (buck_h, buck), (proj_h, proj)]
    loads = [pltpu.make_async_copy(src, dst, load_sem.at[at]) for at, (src, dst) in enumerate(moves)]
    for load in loads:
        load.start()
    load_tok, load_stem = loads[:2]
    load_conv = loads[2 : 2 + kernel]
    load_bias, load_up, load_gain, load_pair, load_outw, load_cot, load_buck, load_proj = loads[2 + kernel :]

    def place(linear):
        return {"seq": lax.div(linear, col_n), "col": lax.rem(linear, col_n), "batch": bat}

    def at(s, c, b):
        return {"seq": s, "col": c, "batch": b}

    def remote(src, dst, send, recv, device):
        return pltpu.make_async_remote_copy(
            src_ref=src,
            dst_ref=dst,
            send_sem=send,
            recv_sem=recv,
            device_id=device,
            device_id_type=MESH,
        )

    barrier = pltpu.get_barrier_semaphore()
    for step in range(1, seq_n * col_n):
        pl.semaphore_signal(
            barrier,
            inc=1,
            device_id=place(lax.rem(me + step, seq_n * col_n)),
            device_id_type=MESH,
        )
    for b_step in range(1, batch_n):
        for c_step in range(col_n):
            pl.semaphore_signal(
                barrier,
                inc=1,
                device_id=at(seq, lax.rem(col + c_step, col_n), lax.rem(bat + b_step, batch_n)),
                device_id_type=MESH,
            )

    spread = (lax.rem(iota((LANES, LANES), 0), PATCH) == lax.div(lax.rem(iota((LANES, LANES), 1), width), BASES)).astype(BF16)

    def expand(lines):
        count = lines.shape[0]
        wide = jnp.broadcast_to(lines.astype(F32)[:, None, :], (count, PAD, LANES)).reshape(count * PAD, LANES)
        own = lax.div(iota(wide.shape, 1), PATCH) == lax.rem(iota(wide.shape, 0), PAD)
        return nn(jnp.where(own, wide, 0.0).astype(BF16), spread)

    load_tok.wait()
    seen[pl.ds(PAD, patches), :] = expand(tok[...])
    mixed[pl.ds(kernel * width, width), :] = jnp.zeros((width, channels), BF16)

    pl.semaphore_wait(barrier, seq_n * col_n - 1 + (batch_n - 1) * col_n)

    lines_n = tok.shape[0]
    to_left = remote(tok.at[pl.ds(0, PAD)], halo_tok.at[1], tok_send.at[0], tok_recv.at[1], place(jnp.maximum(me - 1, 0)))
    to_right = remote(tok.at[pl.ds(lines_n - PAD, PAD)], halo_tok.at[0], tok_send.at[1], tok_recv.at[0], place(jnp.minimum(me + 1, last)))

    @pl.when(me > 0)
    def _():
        to_left.start()

    @pl.when(me < last)
    def _():
        to_right.start()

    load_stem.wait()
    for k in range(kernel):
        load_conv[k].wait()
        mixed[pl.ds(k * width, width), :] = nn(stem[...], conv[pl.ds(k * channels, channels), :]).astype(BF16)

    @pl.when(me > 0)
    def _():
        to_left.wait_send()
        to_right.wait_recv()
        seen[pl.ds(0, PAD), :] = expand(halo_tok[0, PAD - 1 : PAD, :])

    @pl.when(me == 0)
    def _():
        seen[pl.ds(0, PAD), :] = jnp.full((PAD, LANES), -1.0, F32)

    @pl.when(me < last)
    def _():
        to_right.wait_send()
        to_left.wait_recv()
        seen[pl.ds(PAD + patches, PAD), :] = expand(halo_tok[1, 0:1, :])

    @pl.when(me == last)
    def _():
        seen[pl.ds(PAD + patches, PAD), :] = jnp.full((PAD, LANES), -1.0, F32)

    lane = iota((patches, LANES), 1)
    base = lax.rem(lane, BASES).astype(F32)
    for group in range((kernel + 1) // 2):
        first = PAD - reach + 2 * group
        low = seen[pl.ds(first, patches), :]
        if 2 * group + 1 < kernel:
            high = seen[pl.ds(first + 1, patches), :]
        else:
            high = -1.0
        hot[:, group * LANES : (group + 1) * LANES] = jnp.where(jnp.where(lane < width, low, high) == base, 1.0, 0.0).astype(BF16)

    root = 0.7978845608028654
    cube = root * 0.044715

    load_bias.wait()
    shift_row = bias[...][None, :]

    @pl.loop(0, bins)
    def _(b):
        rows = pl.ds(pl.multiple_of(b * POOL, POOL), POOL)
        v = nn(hot[rows, :], mixed[...]) + shift_row
        square = v * v
        t = jnp.tanh(v * (root + cube * square))
        half = 0.5 + 0.5 * t
        pool[pl.ds(b, 1), :] = jnp.sum(v * half, axis=0, keepdims=True) * (1.0 / POOL)
        slope[rows, :] = (half + 0.5 * v * (1.0 - t * t) * (root + 3.0 * cube * square)) * (1.0 / POOL)

    for load in (load_up, load_gain, load_pair):
        load.wait()
    gain_row = gain[...][None, :]
    hidden = nn(pool[...].astype(BF16), up[...])
    inverse = lax.rsqrt(jnp.mean(hidden * hidden, axis=1, keepdims=True) + 1e-06)
    normed = (hidden * inverse * gain_row).astype(BF16)
    lr[...] = jnp.zeros(lr.shape, F32)
    lr[:, : 2 * OP] = nt(normed, pair[...]).astype(BF16).astype(F32)

    user = lax.div(me, seq_n)
    slot = lax.rem(me, seq_n)
    lefts, rights = [], []
    for step in range(1, col_n):
        peer = lax.rem(col + step, col_n)
        lefts.append(remote(lr, got_left.at[col], left_send.at[step], left_recv.at[col], at(seq, peer, bat)))
        lefts[-1].start()
    for s in range(seq_n):
        copy = remote(lr, got_right.at[slot], right_send.at[s], right_recv.at[slot], at(s, user, bat))
        rights.append((copy, (seq != s) | (col != user)))

        @pl.when(rights[-1][1])
        def _():
            copy.start()

    got_left[col] = lr[...]

    @pl.when(col == user)
    def _():
        got_right[slot] = lr[...]

    load_outw.wait()
    load_cot.wait()
    step_rows = 2 * LANES

    @pl.loop(0, rows_n * cols_n // step_rows)
    def _(i):
        rows = pl.ds(pl.multiple_of(i * step_rows, step_rows), step_rows)
        grid[rows, :] = nt(cot[rows, :], outw[...])

    for step in range(1, col_n):
        peer = lax.rem(col + step, col_n)
        remote(lr, got_left.at[peer], left_send.at[step], left_recv.at[peer], at(seq, peer, bat)).wait_recv()
    for s in range(seq_n):
        owner = col * seq_n + s

        @pl.when(owner != me)
        def _():
            remote(lr, got_right.at[s], right_send.at[s], right_recv.at[s], place(owner)).wait_recv()

    for copy in lefts:
        copy.wait_send()
    for copy, other in rights:

        @pl.when(other)
        def _():
            copy.wait_send()

    outer = OP * OP
    pick_left = (iota((LANES, outer), 0) == lax.div(iota((LANES, outer), 1), OP)).astype(BF16)
    pick_right = (iota((LANES, outer), 0) == OP + lax.rem(iota((LANES, outer), 1), OP)).astype(BF16)
    wide_left = nn(got_left[...].reshape(rows_n, LANES).astype(BF16), pick_left)
    wide_right = nn(got_right[...].reshape(cols_n, LANES).astype(BF16), pick_right)
    over_cols, over_rows = [], []
    for tile in range(outer // LANES):
        lanes = slice(tile * LANES, (tile + 1) * LANES)
        cells = grid[:, lanes].reshape(rows_n, cols_n, LANES)
        over_cols.append(jnp.sum(cells * wide_right[None, :, lanes], axis=1))
        over_rows.append(jnp.sum(cells * wide_left[:, None, lanes], axis=0))
    part_left[...] = joined(nt(halves(jnp.concatenate(over_cols, axis=1)), pick_left))
    part_right[...] = joined(nt(halves(jnp.concatenate(over_rows, axis=1)), pick_right))

    lefts, rights = [], []
    for step in range(1, col_n):
        peer = lax.rem(col + step, col_n)
        piece = part_left.at[pl.ds(pl.multiple_of(peer * bins, bins), bins)]
        lefts.append(remote(piece, sum_left.at[col], gl_send.at[step], gl_recv.at[col], at(seq, peer, bat)))
        lefts[-1].start()
    for s in range(seq_n):
        owner = col * seq_n + s
        copy = remote(part_right.at[pl.ds(s * bins, bins)], sum_right.at[seq], gr_send.at[s], gr_recv.at[seq], place(owner))
        rights.append((copy, owner != me))

        @pl.when(owner != me)
        def _():
            copy.start()

        @pl.when(owner == me)
        def _():
            sum_right[seq] = part_right[s * bins : (s + 1) * bins, :]

    sum_left[col] = part_left[pl.ds(pl.multiple_of(col * bins, bins), bins), :]

    load_buck.wait()
    member = (buck[...][None, :] == iota((BUCKETS, kernel * channels), 0)).astype(BF16)
    stems = [nt(member[:, k * channels : (k + 1) * channels], stem[...]) for k in range(kernel)]
    stems.append(jnp.zeros((BUCKETS, width), F32))
    marks[...] = halves(joined(nt(halves(jnp.concatenate(stems, axis=1)), hot[...])))

    for step in range(1, col_n):
        peer = lax.rem(col + step, col_n)
        remote(lr, sum_left.at[peer], gl_send.at[step], gl_recv.at[peer], at(seq, peer, bat)).wait_recv()
    for s in range(seq_n):

        @pl.when((seq != s) | (col != user))
        def _():
            remote(lr, sum_right.at[s], gr_send.at[s], gr_recv.at[s], at(s, user, bat)).wait_recv()

    both = jnp.sum(sum_left[...], axis=0) + jnp.sum(sum_right[...], axis=0)
    d_normed = joined(nn(halves(both[:, : 2 * OP]), pair[...]))
    scaled = d_normed * gain_row
    inner = jnp.mean(scaled * hidden, axis=1, keepdims=True)
    d_hidden = inverse * scaled - hidden * (inverse * inverse * inverse) * inner
    pool[...] = joined(nt(halves(d_hidden), up[...]))

    dpad[pl.ds(PAD, PAD), :] = slope[:PAD, :] * pool[0:1, :]
    dpad[pl.ds(patches, PAD), :] = slope[patches - PAD :, :] * pool[bins - 1 : bins, :]
    edge_left = remote(dpad.at[pl.ds(PAD, PAD)], dpad.at[pl.ds(PAD + patches, PAD)], edge_send.at[0], edge_recv.at[1], place(jnp.maximum(me - 1, 0)))
    edge_right = remote(dpad.at[pl.ds(patches, PAD)], dpad.at[pl.ds(0, PAD)], edge_send.at[1], edge_recv.at[0], place(jnp.minimum(me + 1, last)))

    @pl.when(me > 0)
    def _():
        edge_left.start()

    @pl.when(me < last)
    def _():
        edge_right.start()

    @pl.when(me == 0)
    def _():
        dpad[pl.ds(0, PAD), :] = jnp.zeros((PAD, channels), F32)

    @pl.when(me == last)
    def _():
        dpad[pl.ds(PAD + patches, PAD), :] = jnp.zeros((PAD, channels), F32)

    for copy in lefts:
        copy.wait_send()
    for copy, other in rights:

        @pl.when(other)
        def _():
            copy.wait_send()

    total = jnp.zeros((2 * BUCKETS, channels), F32)
    for b in range(bins):
        first = b * POOL
        cells = slope[first : first + POOL, :] * pool[b : b + 1, :]
        low = PAD if b == 0 else 0
        high = POOL - PAD if b == bins - 1 else POOL
        dpad[pl.ds(PAD + first + low, high - low), :] = cells[low:high]
        total = total + nn(marks[:, first : first + POOL], cells.astype(BF16))
    load_proj.wait()
    sk[...] = lax.dot_general(
        joined(total), proj[...], (((1,), (0,)), ((), ())), precision=lax.Precision.HIGHEST, preferred_element_type=F32
    )
    share = BUCKETS // col_n

    sends_a = []
    for step in range(1, col_n):
        peer = lax.rem(col + step, col_n)
        piece = sk.at[pl.ds(pl.multiple_of(peer * share, share), share)]
        sends_a.append(remote(piece, sk_a.at[col], a_send.at[step], a_recv.at[col], at(seq, peer, bat)))
        sends_a[-1].start()
    sk_a[col] = sk[pl.ds(pl.multiple_of(col * share, share), share), :]
    sends_b = [
        remote(sk_bsrc, sk_b.at[seq], b_send.at[step], b_recv.at[seq], at(lax.rem(seq + step, seq_n), col, bat))
        for step in range(1, seq_n)
    ]
    pairs = [(b, c) for b in range(batch_n) for c in range(col_n) if b + c > 0]
    sends_c = [
        remote(
            sk_csrc,
            sk_c.at[bat, col],
            c_send.at[b, c],
            c_recv.at[bat, col],
            at(seq, lax.rem(col + c, col_n), lax.rem(bat + b, batch_n)),
        )
        for b, c in pairs
    ]

    chunk = 2 * LANES
    chunks = patches // chunk

    @pl.loop(0, chunks)
    def _(i):
        @pl.when(i == 1)
        def _():
            for step in range(1, col_n):
                peer = lax.rem(col + step, col_n)
                remote(sk_bsrc, sk_a.at[peer], a_send.at[step], a_recv.at[peer], at(seq, peer, bat)).wait_recv()
            sk_bsrc[...] = jnp.sum(sk_a[...], axis=0)
            sk_b[seq] = jnp.sum(sk_a[...], axis=0)
            for copy in sends_b:
                copy.start()

        @pl.when(i == 2)
        def _():
            for step in range(1, seq_n):
                peer = lax.rem(seq + step, seq_n)
                remote(sk_bsrc, sk_b.at[peer], b_send.at[step], b_recv.at[peer], at(peer, col, bat)).wait_recv()
            sk_csrc[...] = jnp.sum(sk_b[...], axis=0)
            sk_c[bat, col] = jnp.sum(sk_b[...], axis=0)
            for copy in sends_c:
                copy.start()

            @pl.when(me > 0)
            def _():
                edge_left.wait_send()
                edge_right.wait_recv()

            @pl.when(me < last)
            def _():
                edge_right.wait_send()
                edge_left.wait_recv()

        spot = lax.rem(i + 1, chunks)
        begin = pl.multiple_of(spot * chunk, chunk)
        wide = dpad[pl.ds(begin, chunk + 2 * PAD), :]
        acc = jnp.zeros((chunk, channels), F32)
        for k in range(kernel):
            shift = PAD + reach - k
            acc = acc + nt(wide[shift : shift + chunk].astype(BF16), conv[pl.ds(k * channels, channels), :])
        outv[pl.ds(begin, chunk), :] = acc.astype(BF16)
        pltpu.make_async_copy(outv.at[pl.ds(begin, chunk)], out_h.at[pl.ds(begin, chunk)], store_sem.at[spot]).start()

    for b, c in pairs:
        other_b, other_c = lax.rem(bat + b, batch_n), lax.rem(col + c, col_n)
        remote(sk_csrc, sk_c.at[other_b, other_c], c_send.at[b, c], c_recv.at[other_b, other_c], at(seq, other_c, other_b)).wait_recv()

    def unit(values):
        values = values.reshape(BUCKETS, values.shape[-1])
        return values * lax.rsqrt(jnp.mean(values * values) + 1e-06)

    center = unit(sk_c[0])
    for b in range(1, batch_n):
        center = center + unit(sk_c[b])
    emb[...] = unit(sk_c[bat]) - center * (1.0 / batch_n)
    for copy in sends_a + sends_b + sends_c:
        copy.wait_send()
    for i in range(chunks):
        rows = pl.ds(i * chunk, chunk)
        pltpu.make_async_copy(outv.at[rows], out_h.at[rows], store_sem.at[i]).wait()


def shards(
    tokens,
    stem_weight,
    conv_weight,
    conv_bias,
    up_weight,
    norm_gain,
    pair_weight,
    out_weight,
    cotangent,
    projection,
    buckets,
):
    seq_n, col_n, batch_n = (lax.axis_size(axis) for axis in ("seq", "col", "batch"))
    channels = conv_weight.shape[1]
    kernel = conv_weight.shape[0] // channels
    patches = tokens.shape[1] // PATCH
    bins = patches // POOL
    rows_n, cols_n = bins * col_n, bins * seq_n
    proj_n = projection.shape[1]
    share = BUCKETS // col_n
    hot_n = (kernel + 1) // 2 * LANES
    vmem = pl.BlockSpec(memory_space=pltpu.VMEM)
    hbm = pl.BlockSpec(memory_space=pl.ANY)
    dma = pltpu.SemaphoreType.DMA
    cot = cotangent.reshape(rows_n * cols_n, cotangent.shape[3])
    scratch = [
        pltpu.VMEM((patches * PATCH // LANES, LANES), jnp.int32),
        pltpu.VMEM(stem_weight.shape, BF16),
        pltpu.VMEM(conv_bias.shape, F32),
        pltpu.VMEM(norm_gain.shape, F32),
        pltpu.VMEM(pair_weight.shape[::-1], BF16),
        pltpu.VMEM(projection.shape, F32),
        pltpu.VMEM(buckets.shape, jnp.int32),
        pltpu.VMEM(conv_weight.shape, BF16),
        pltpu.VMEM(up_weight.shape, BF16),
        pltpu.VMEM(out_weight.shape, BF16),
        pltpu.VMEM(cot.shape, BF16),
        pltpu.VMEM((rows_n * cols_n, OP * OP), F32),
        pltpu.VMEM((patches + 2 * PAD, LANES), F32),
        pltpu.VMEM((patches, hot_n), BF16),
        pltpu.VMEM((hot_n, channels), BF16),
        pltpu.VMEM((patches, channels), F32),
        pltpu.VMEM((bins, channels), F32),
        pltpu.VMEM((patches + 2 * PAD, channels), F32),
        pltpu.VMEM((patches, channels), BF16),
        pltpu.VMEM((2, PAD, LANES), jnp.int32),
        pltpu.VMEM((bins, LANES), F32),
        pltpu.VMEM((col_n, bins, LANES), F32),
        pltpu.VMEM((seq_n, bins, LANES), F32),
        pltpu.VMEM((rows_n, LANES), F32),
        pltpu.VMEM((cols_n, LANES), F32),
        pltpu.VMEM((col_n, bins, LANES), F32),
        pltpu.VMEM((seq_n, bins, LANES), F32),
        pltpu.VMEM((2 * BUCKETS, patches), BF16),
        pltpu.VMEM((BUCKETS, proj_n), F32),
        pltpu.VMEM((col_n, share, proj_n), F32),
        pltpu.VMEM((seq_n, share, proj_n), F32),
        pltpu.VMEM((share, proj_n), F32),
        pltpu.VMEM((batch_n, col_n, share, proj_n), F32),
        pltpu.VMEM((share, proj_n), F32),
        dma((10 + kernel,)),
        dma((patches // (2 * LANES),)),
        dma((2,)),
        dma((2,)),
        dma((col_n,)),
        dma((col_n,)),
        dma((seq_n,)),
        dma((seq_n,)),
        dma((col_n,)),
        dma((col_n,)),
        dma((seq_n,)),
        dma((seq_n,)),
        dma((2,)),
        dma((2,)),
        dma((col_n,)),
        dma((col_n,)),
        dma((seq_n,)),
        dma((seq_n,)),
        dma((batch_n, col_n)),
        dma((batch_n, col_n)),
    ]
    input_grad, embedding = pl.pallas_call(
        functools.partial(body, (seq_n, col_n, batch_n)),
        out_shape=(
            jax.ShapeDtypeStruct((patches, channels), BF16),
            jax.ShapeDtypeStruct((BUCKETS, proj_n), F32),
        ),
        in_specs=[hbm] * 11,
        out_specs=(hbm, vmem),
        scratch_shapes=scratch,
        compiler_params=pltpu.CompilerParams(
            collective_id=0, has_side_effects=True, vmem_limit_bytes=56 * 2**20
        ),
    )(
        tokens.reshape(patches * PATCH // LANES, LANES),
        stem_weight,
        conv_bias,
        norm_gain,
        pair_weight.T,
        projection,
        buckets,
        conv_weight,
        up_weight,
        out_weight,
        cot,
    )
    return (input_grad[None], embedding[None])


def solution(mesh):
    in_specs = (
        P("batch", ("seq", "col")),
        P(),
        P(),
        P(),
        P(),
        P(),
        P(),
        P(),
        P("batch", "seq", "col", None),
        P(),
        P(),
    )
    out_specs = (P("batch", ("seq", "col"), None), P("batch", None, None))
    return jax.shard_map(shards, mesh=mesh, in_specs=in_specs, out_specs=out_specs, check_vma=False)
```

```python
import functools

import jax
import jax.numpy as jnp
from jax import lax
from jax.experimental import pallas as pl
from jax.experimental.pallas import tpu as pltpu
from jax.sharding import PartitionSpec as P

OP = 32
PATCH = 16
POOL = 128
BUCKETS = 32
BASES = 4
LANES = 128
PAD = 8

MESH = pl.DeviceIdType.MESH
F32 = jnp.float32
BF16 = jnp.bfloat16


def nn(a, b):
    return lax.dot_general(a, b, (((1,), (0,)), ((), ())), preferred_element_type=F32)


def nt(a, b):
    return lax.dot_general(a, b, (((1,), (1,)), ((), ())), preferred_element_type=F32)


def halves(values):
    upper = values.astype(BF16)
    lower = (values - upper.astype(F32)).astype(BF16)
    return jnp.concatenate([upper, lower], axis=0)


def joined(values):
    rows = values.shape[0] // 2
    return values[:rows] + values[rows:]


def iota(shape, dim):
    return lax.broadcasted_iota(jnp.int32, shape, dim)


def body(
    counts,
    tok_h,
    stem_h,
    bias_h,
    gain_h,
    pair_h,
    proj_h,
    buck_h,
    conv_h,
    up_h,
    outw_h,
    cot_h,
    out_h,
    emb,
    tok,
    stem,
    bias,
    gain,
    pair,
    proj,
    buck,
    conv,
    up,
    outw,
    cot,
    grid,
    seen,
    hot,
    mixed,
    slope,
    pool,
    dpad,
    outv,
    halo_tok,
    lr,
    got_left,
    got_right,
    part_left,
    part_right,
    sum_left,
    sum_right,
    marks,
    sk,
    sk_a,
    sk_b,
    sk_bsrc,
    sk_c,
    sk_csrc,
    load_sem,
    store_sem,
    tok_send,
    tok_recv,
    left_send,
    left_recv,
    right_send,
    right_recv,
    gl_send,
    gl_recv,
    gr_send,
    gr_recv,
    edge_send,
    edge_recv,
    a_send,
    a_recv,
    b_send,
    b_recv,
    c_send,
    c_recv,
):
    seq_n, col_n, batch_n = counts
    seq, col, bat = lax.axis_index("seq"), lax.axis_index("col"), lax.axis_index("batch")
    me = seq * col_n + col
    last = seq_n * col_n - 1
    channels = conv.shape[1]
    kernel = conv.shape[0] // channels
    reach = (kernel - 1) // 2
    patches = slope.shape[0]
    bins = patches // POOL
    width = stem.shape[0]
    rows_n, cols_n = bins * col_n, bins * seq_n

    taps = [pl.ds(k * channels, channels) for k in range(kernel)]
    moves = [(tok_h, tok), (stem_h, stem), (buck_h, buck), (outw_h, outw), (cot_h, cot)]
    moves += [(conv_h.at[tap], conv.at[tap]) for tap in taps]
    moves += [(bias_h, bias), (up_h, up), (gain_h, gain), (pair_h, pair), (proj_h, proj)]
    loads = [pltpu.make_async_copy(src, dst, load_sem.at[at]) for at, (src, dst) in enumerate(moves)]
    for load in loads:
        load.start()
    load_tok, load_stem, load_buck, load_outw, load_cot = loads[:5]
    load_conv = loads[5 : 5 + kernel]
    load_bias, load_up, load_gain, load_pair, load_proj = loads[5 + kernel :]

    def place(linear):
        return {"seq": lax.div(linear, col_n), "col": lax.rem(linear, col_n), "batch": bat}

    def at(s, c, b):
        return {"seq": s, "col": c, "batch": b}

    def remote(src, dst, send, recv, device):
        return pltpu.make_async_remote_copy(
            src_ref=src,
            dst_ref=dst,
            send_sem=send,
            recv_sem=recv,
            device_id=device,
            device_id_type=MESH,
        )

    barrier = pltpu.get_barrier_semaphore()
    for step in range(1, seq_n * col_n):
        pl.semaphore_signal(
            barrier,
            inc=1,
            device_id=place(lax.rem(me + step, seq_n * col_n)),
            device_id_type=MESH,
        )
    for b_step in range(1, batch_n):
        for c_step in range(col_n):
            pl.semaphore_signal(
                barrier,
                inc=1,
                device_id=at(seq, lax.rem(col + c_step, col_n), lax.rem(bat + b_step, batch_n)),
                device_id_type=MESH,
            )

    spread = (lax.rem(iota((LANES, LANES), 0), PATCH) == lax.div(lax.rem(iota((LANES, LANES), 1), width), BASES)).astype(BF16)

    def expand(lines):
        count = lines.shape[0]
        wide = jnp.broadcast_to(lines.astype(F32)[:, None, :], (count, PAD, LANES)).reshape(count * PAD, LANES)
        own = lax.div(iota(wide.shape, 1), PATCH) == lax.rem(iota(wide.shape, 0), PAD)
        return nn(jnp.where(own, wide, 0.0).astype(BF16), spread)

    load_tok.wait()
    seen[pl.ds(PAD, patches), :] = expand(tok[...])
    mixed[pl.ds(kernel * width, width), :] = jnp.zeros((width, channels), BF16)

    load_stem.wait()
    load_buck.wait()
    member = (buck[...][None, :] == iota((BUCKETS, kernel * channels), 0)).astype(BF16)
    stems = [nt(member[:, k * channels : (k + 1) * channels], stem[...]) for k in range(kernel)]
    stems.append(jnp.zeros((BUCKETS, width), F32))
    stem_marks = halves(jnp.concatenate(stems, axis=1))

    load_outw.wait()
    load_cot.wait()
    step_rows = 2 * LANES

    @pl.loop(0, rows_n * cols_n // step_rows)
    def _(i):
        rows = pl.ds(pl.multiple_of(i * step_rows, step_rows), step_rows)
        grid[rows, :] = nt(cot[rows, :], outw[...])

    pl.semaphore_wait(barrier, seq_n * col_n - 1 + (batch_n - 1) * col_n)

    lines_n = tok.shape[0]
    to_left = remote(tok.at[pl.ds(0, PAD)], halo_tok.at[1], tok_send.at[0], tok_recv.at[1], place(jnp.maximum(me - 1, 0)))
    to_right = remote(tok.at[pl.ds(lines_n - PAD, PAD)], halo_tok.at[0], tok_send.at[1], tok_recv.at[0], place(jnp.minimum(me + 1, last)))

    @pl.when(me > 0)
    def _():
        to_left.start()

    @pl.when(me < last)
    def _():
        to_right.start()

    for k in range(kernel):
        load_conv[k].wait()
        mixed[pl.ds(k * width, width), :] = nn(stem[...], conv[pl.ds(k * channels, channels), :]).astype(BF16)

    def encode(first, count):
        lane = iota((count, LANES), 1)
        base = lax.rem(lane, BASES).astype(F32)
        for group in range((kernel + 1) // 2):
            spot = first + PAD - reach + 2 * group
            low = seen[pl.ds(spot, count), :]
            if 2 * group + 1 < kernel:
                high = seen[pl.ds(spot + 1, count), :]
            else:
                high = -1.0
            match = jnp.where(lane < width, low, high) == base
            hot[first : first + count, group * LANES : (group + 1) * LANES] = jnp.where(match, 1.0, 0.0).astype(BF16)

    root = 0.7978845608028654
    cube = root * 0.044715
    load_bias.wait()
    shift_row = bias[...][None, :]

    def forward(b):
        rows = pl.ds(pl.multiple_of(b * POOL, POOL), POOL)
        v = nn(hot[rows, :], mixed[...]) + shift_row
        square = v * v
        t = jnp.tanh(v * (root + cube * square))
        half = 0.5 + 0.5 * t
        pool[pl.ds(b, 1), :] = jnp.sum(v * half, axis=0, keepdims=True) * (1.0 / POOL)
        slope[rows, :] = (half + 0.5 * v * (1.0 - t * t) * (root + 3.0 * cube * square)) * (1.0 / POOL)

    encode(POOL, patches - 2 * POOL)
    pl.loop(1, bins - 1)(forward)

    @pl.when(me > 0)
    def _():
        to_left.wait_send()
        to_right.wait_recv()
        seen[pl.ds(0, PAD), :] = expand(halo_tok[0, PAD - 1 : PAD, :])

    @pl.when(me == 0)
    def _():
        seen[pl.ds(0, PAD), :] = jnp.full((PAD, LANES), -1.0, F32)

    @pl.when(me < last)
    def _():
        to_right.wait_send()
        to_left.wait_recv()
        seen[pl.ds(PAD + patches, PAD), :] = expand(halo_tok[1, 0:1, :])

    @pl.when(me == last)
    def _():
        seen[pl.ds(PAD + patches, PAD), :] = jnp.full((PAD, LANES), -1.0, F32)

    encode(0, POOL)
    encode(patches - POOL, POOL)

    @pl.loop(0, 2)
    def _(side):
        forward(side * (bins - 1))

    for load in (load_up, load_gain, load_pair):
        load.wait()
    gain_row = gain[...][None, :]
    hidden = nn(pool[...].astype(BF16), up[...])
    inverse = lax.rsqrt(jnp.mean(hidden * hidden, axis=1, keepdims=True) + 1e-06)
    normed = (hidden * inverse * gain_row).astype(BF16)
    lr[...] = jnp.zeros(lr.shape, F32)
    lr[:, : 2 * OP] = nt(normed, pair[...]).astype(BF16).astype(F32)

    user = lax.div(me, seq_n)
    slot = lax.rem(me, seq_n)
    lefts, rights = [], []
    for step in range(1, col_n):
        peer = lax.rem(col + step, col_n)
        lefts.append(remote(lr, got_left.at[col], left_send.at[step], left_recv.at[col], at(seq, peer, bat)))
        lefts[-1].start()
    for s in range(seq_n):
        copy = remote(lr, got_right.at[slot], right_send.at[s], right_recv.at[slot], at(s, user, bat))
        rights.append((copy, (seq != s) | (col != user)))

        @pl.when(rights[-1][1])
        def _():
            copy.start()

    got_left[col] = lr[...]

    @pl.when(col == user)
    def _():
        got_right[slot] = lr[...]

    marks[...] = halves(joined(nt(stem_marks, hot[...])))

    for step in range(1, col_n):
        peer = lax.rem(col + step, col_n)
        remote(lr, got_left.at[peer], left_send.at[step], left_recv.at[peer], at(seq, peer, bat)).wait_recv()
    for s in range(seq_n):
        owner = col * seq_n + s

        @pl.when(owner != me)
        def _():
            remote(lr, got_right.at[s], right_send.at[s], right_recv.at[s], place(owner)).wait_recv()

    for copy in lefts:
        copy.wait_send()
    for copy, other in rights:

        @pl.when(other)
        def _():
            copy.wait_send()

    outer = OP * OP
    pick_left = (iota((LANES, outer), 0) == lax.div(iota((LANES, outer), 1), OP)).astype(BF16)
    pick_right = (iota((LANES, outer), 0) == OP + lax.rem(iota((LANES, outer), 1), OP)).astype(BF16)
    wide_left = nn(got_left[...].reshape(rows_n, LANES).astype(BF16), pick_left)
    wide_right = nn(got_right[...].reshape(cols_n, LANES).astype(BF16), pick_right)
    over_cols, over_rows = [], []
    for tile in range(outer // LANES):
        lanes = slice(tile * LANES, (tile + 1) * LANES)
        cells = grid[:, lanes].reshape(rows_n, cols_n, LANES)
        over_cols.append(jnp.sum(cells * wide_right[None, :, lanes], axis=1))
        over_rows.append(jnp.sum(cells * wide_left[:, None, lanes], axis=0))
    part_left[...] = joined(nt(halves(jnp.concatenate(over_cols, axis=1)), pick_left))
    part_right[...] = joined(nt(halves(jnp.concatenate(over_rows, axis=1)), pick_right))

    lefts, rights = [], []
    for step in range(1, col_n):
        peer = lax.rem(col + step, col_n)
        piece = part_left.at[pl.ds(pl.multiple_of(peer * bins, bins), bins)]
        lefts.append(remote(piece, sum_left.at[col], gl_send.at[step], gl_recv.at[col], at(seq, peer, bat)))
        lefts[-1].start()
    for s in range(seq_n):
        owner = col * seq_n + s
        copy = remote(part_right.at[pl.ds(s * bins, bins)], sum_right.at[seq], gr_send.at[s], gr_recv.at[seq], place(owner))
        rights.append((copy, owner != me))

        @pl.when(owner != me)
        def _():
            copy.start()

        @pl.when(owner == me)
        def _():
            sum_right[seq] = part_right[s * bins : (s + 1) * bins, :]

    sum_left[col] = part_left[pl.ds(pl.multiple_of(col * bins, bins), bins), :]

    for step in range(1, col_n):
        peer = lax.rem(col + step, col_n)
        remote(lr, sum_left.at[peer], gl_send.at[step], gl_recv.at[peer], at(seq, peer, bat)).wait_recv()
    for s in range(seq_n):

        @pl.when((seq != s) | (col != user))
        def _():
            remote(lr, sum_right.at[s], gr_send.at[s], gr_recv.at[s], at(s, user, bat)).wait_recv()

    both = jnp.sum(sum_left[...], axis=0) + jnp.sum(sum_right[...], axis=0)
    d_normed = joined(nn(halves(both[:, : 2 * OP]), pair[...]))
    scaled = d_normed * gain_row
    inner = jnp.mean(scaled * hidden, axis=1, keepdims=True)
    d_hidden = inverse * scaled - hidden * (inverse * inverse * inverse) * inner
    pool[...] = joined(nt(halves(d_hidden), up[...]))

    dpad[pl.ds(PAD, PAD), :] = slope[:PAD, :] * pool[0:1, :]
    dpad[pl.ds(patches, PAD), :] = slope[patches - PAD :, :] * pool[bins - 1 : bins, :]
    edge_left = remote(dpad.at[pl.ds(PAD, PAD)], dpad.at[pl.ds(PAD + patches, PAD)], edge_send.at[0], edge_recv.at[1], place(jnp.maximum(me - 1, 0)))
    edge_right = remote(dpad.at[pl.ds(patches, PAD)], dpad.at[pl.ds(0, PAD)], edge_send.at[1], edge_recv.at[0], place(jnp.minimum(me + 1, last)))

    @pl.when(me > 0)
    def _():
        edge_left.start()

    @pl.when(me < last)
    def _():
        edge_right.start()

    @pl.when(me == 0)
    def _():
        dpad[pl.ds(0, PAD), :] = jnp.zeros((PAD, channels), F32)

    @pl.when(me == last)
    def _():
        dpad[pl.ds(PAD + patches, PAD), :] = jnp.zeros((PAD, channels), F32)

    for copy in lefts:
        copy.wait_send()
    for copy, other in rights:

        @pl.when(other)
        def _():
            copy.wait_send()

    for b in range(bins):
        first = b * POOL
        cells = slope[first : first + POOL, :] * pool[b : b + 1, :]
        low = PAD if b == 0 else 0
        high = POOL - PAD if b == bins - 1 else POOL
        dpad[pl.ds(PAD + first + low, high - low), :] = cells[low:high]
    sums = joined(nn(marks[...], dpad[pl.ds(PAD, patches), :].astype(BF16)))
    load_proj.wait()
    proj_high = proj[...].astype(BF16)
    proj_low = (proj[...] - proj_high.astype(F32)).astype(BF16)
    sk[...] = joined(nn(halves(sums), proj_high)) + nn(sums.astype(BF16), proj_low)

    share = BUCKETS // col_n

    sends_a = []
    for step in range(1, col_n):
        peer = lax.rem(col + step, col_n)
        piece = sk.at[pl.ds(pl.multiple_of(peer * share, share), share)]
        sends_a.append(remote(piece, sk_a.at[col], a_send.at[step], a_recv.at[col], at(seq, peer, bat)))
        sends_a[-1].start()
    sk_a[col] = sk[pl.ds(pl.multiple_of(col * share, share), share), :]
    sends_b = [
        remote(sk_bsrc, sk_b.at[seq], b_send.at[step], b_recv.at[seq], at(lax.rem(seq + step, seq_n), col, bat))
        for step in range(1, seq_n)
    ]
    pairs = [(b, c) for b in range(batch_n) for c in range(col_n) if b + c > 0]
    sends_c = [
        remote(
            sk_csrc,
            sk_c.at[bat, col],
            c_send.at[b, c],
            c_recv.at[bat, col],
            at(seq, lax.rem(col + c, col_n), lax.rem(bat + b, batch_n)),
        )
        for b, c in pairs
    ]

    chunk = 2 * LANES
    chunks = patches // chunk

    @pl.loop(0, chunks)
    def _(i):
        @pl.when(i == 1)
        def _():
            for step in range(1, col_n):
                peer = lax.rem(col + step, col_n)
                remote(sk_bsrc, sk_a.at[peer], a_send.at[step], a_recv.at[peer], at(seq, peer, bat)).wait_recv()
            sk_bsrc[...] = jnp.sum(sk_a[...], axis=0)
            sk_b[seq] = jnp.sum(sk_a[...], axis=0)
            for copy in sends_b:
                copy.start()

        @pl.when(i == 2)
        def _():
            for step in range(1, seq_n):
                peer = lax.rem(seq + step, seq_n)
                remote(sk_bsrc, sk_b.at[peer], b_send.at[step], b_recv.at[peer], at(peer, col, bat)).wait_recv()
            sk_csrc[...] = jnp.sum(sk_b[...], axis=0)
            sk_c[bat, col] = jnp.sum(sk_b[...], axis=0)
            for copy in sends_c:
                copy.start()

            @pl.when(me > 0)
            def _():
                edge_left.wait_send()
                edge_right.wait_recv()

            @pl.when(me < last)
            def _():
                edge_right.wait_send()
                edge_left.wait_recv()

        spot = lax.rem(i + 1, chunks)
        begin = pl.multiple_of(spot * chunk, chunk)
        wide = dpad[pl.ds(begin, chunk + 2 * PAD), :]
        acc = jnp.zeros((chunk, channels), F32)
        for k in range(kernel):
            shift = PAD + reach - k
            acc = acc + nt(wide[shift : shift + chunk].astype(BF16), conv[pl.ds(k * channels, channels), :])
        outv[pl.ds(begin, chunk), :] = acc.astype(BF16)
        pltpu.make_async_copy(outv.at[pl.ds(begin, chunk)], out_h.at[pl.ds(begin, chunk)], store_sem.at[spot]).start()

    for b, c in pairs:
        other_b, other_c = lax.rem(bat + b, batch_n), lax.rem(col + c, col_n)
        remote(sk_csrc, sk_c.at[other_b, other_c], c_send.at[b, c], c_recv.at[other_b, other_c], at(seq, other_c, other_b)).wait_recv()

    def unit(values):
        values = values.reshape(BUCKETS, values.shape[-1])
        return values * lax.rsqrt(jnp.mean(values * values) + 1e-06)

    center = unit(sk_c[0])
    for b in range(1, batch_n):
        center = center + unit(sk_c[b])
    emb[...] = unit(sk_c[bat]) - center * (1.0 / batch_n)
    for copy in sends_a + sends_b + sends_c:
        copy.wait_send()
    for i in range(chunks):
        rows = pl.ds(i * chunk, chunk)
        pltpu.make_async_copy(outv.at[rows], out_h.at[rows], store_sem.at[i]).wait()


def shards(
    tokens,
    stem_weight,
    conv_weight,
    conv_bias,
    up_weight,
    norm_gain,
    pair_weight,
    out_weight,
    cotangent,
    projection,
    buckets,
):
    seq_n, col_n, batch_n = (lax.axis_size(axis) for axis in ("seq", "col", "batch"))
    channels = conv_weight.shape[1]
    kernel = conv_weight.shape[0] // channels
    patches = tokens.shape[1] // PATCH
    bins = patches // POOL
    rows_n, cols_n = bins * col_n, bins * seq_n
    proj_n = projection.shape[1]
    share = BUCKETS // col_n
    hot_n = (kernel + 1) // 2 * LANES
    vmem = pl.BlockSpec(memory_space=pltpu.VMEM)
    hbm = pl.BlockSpec(memory_space=pl.ANY)
    dma = pltpu.SemaphoreType.DMA
    cot = cotangent.reshape(rows_n * cols_n, cotangent.shape[3])
    scratch = [
        pltpu.VMEM((patches * PATCH // LANES, LANES), jnp.int32),
        pltpu.VMEM(stem_weight.shape, BF16),
        pltpu.VMEM(conv_bias.shape, F32),
        pltpu.VMEM(norm_gain.shape, F32),
        pltpu.VMEM(pair_weight.shape[::-1], BF16),
        pltpu.VMEM(projection.shape, F32),
        pltpu.VMEM(buckets.shape, jnp.int32),
        pltpu.VMEM(conv_weight.shape, BF16),
        pltpu.VMEM(up_weight.shape, BF16),
        pltpu.VMEM(out_weight.shape, BF16),
        pltpu.VMEM(cot.shape, BF16),
        pltpu.VMEM((rows_n * cols_n, OP * OP), F32),
        pltpu.VMEM((patches + 2 * PAD, LANES), F32),
        pltpu.VMEM((patches, hot_n), BF16),
        pltpu.VMEM((hot_n, channels), BF16),
        pltpu.VMEM((patches, channels), F32),
        pltpu.VMEM((bins, channels), F32),
        pltpu.VMEM((patches + 2 * PAD, channels), F32),
        pltpu.VMEM((patches, channels), BF16),
        pltpu.VMEM((2, PAD, LANES), jnp.int32),
        pltpu.VMEM((bins, LANES), F32),
        pltpu.VMEM((col_n, bins, LANES), F32),
        pltpu.VMEM((seq_n, bins, LANES), F32),
        pltpu.VMEM((rows_n, LANES), F32),
        pltpu.VMEM((cols_n, LANES), F32),
        pltpu.VMEM((col_n, bins, LANES), F32),
        pltpu.VMEM((seq_n, bins, LANES), F32),
        pltpu.VMEM((2 * BUCKETS, patches), BF16),
        pltpu.VMEM((BUCKETS, proj_n), F32),
        pltpu.VMEM((col_n, share, proj_n), F32),
        pltpu.VMEM((seq_n, share, proj_n), F32),
        pltpu.VMEM((share, proj_n), F32),
        pltpu.VMEM((batch_n, col_n, share, proj_n), F32),
        pltpu.VMEM((share, proj_n), F32),
        dma((10 + kernel,)),
        dma((patches // (2 * LANES),)),
        dma((2,)),
        dma((2,)),
        dma((col_n,)),
        dma((col_n,)),
        dma((seq_n,)),
        dma((seq_n,)),
        dma((col_n,)),
        dma((col_n,)),
        dma((seq_n,)),
        dma((seq_n,)),
        dma((2,)),
        dma((2,)),
        dma((col_n,)),
        dma((col_n,)),
        dma((seq_n,)),
        dma((seq_n,)),
        dma((batch_n, col_n)),
        dma((batch_n, col_n)),
    ]
    input_grad, embedding = pl.pallas_call(
        functools.partial(body, (seq_n, col_n, batch_n)),
        out_shape=(
            jax.ShapeDtypeStruct((patches, channels), BF16),
            jax.ShapeDtypeStruct((BUCKETS, proj_n), F32),
        ),
        in_specs=[hbm] * 11,
        out_specs=(hbm, vmem),
        scratch_shapes=scratch,
        compiler_params=pltpu.CompilerParams(
            collective_id=0, has_side_effects=True, vmem_limit_bytes=56 * 2**20
        ),
    )(
        tokens.reshape(patches * PATCH // LANES, LANES),
        stem_weight,
        conv_bias,
        norm_gain,
        pair_weight.T,
        projection,
        buckets,
        conv_weight,
        up_weight,
        out_weight,
        cot,
    )
    return (input_grad[None], embedding[None])


def solution(mesh):
    in_specs = (
        P("batch", ("seq", "col")),
        P(),
        P(),
        P(),
        P(),
        P(),
        P(),
        P(),
        P("batch", "seq", "col", None),
        P(),
        P(),
    )
    out_specs = (P("batch", ("seq", "col"), None), P("batch", None, None))
    return jax.shard_map(shards, mesh=mesh, in_specs=in_specs, out_specs=out_specs, check_vma=False)
```
